256 devices in a mesh: gx: 32 (over x, y, core), gy: 8 (over z).
Axes of the slice: x: 4, y: 4, z: 8, core: 2. Of those that a mesh axis runs over, the one named last changes fastest.
Arguments:
- value: float32 [8, 2048, 8192], P(None, 'gx', 'gy'), may hold values from -6 to 6
- kernel_rows: float32 [511], replicated, may hold values from 0.0009784736 to 0.0029354207
- kernel_cols: float32 [511], replicated, may hold values from 0.0009784736 to 0.0029354207
- intensity: float32 [2], replicated, may hold values from 0.02 to 0.1
- diffusion: float32 [3], replicated, may hold values from 0.02 to 0.1
- drift: float32 [3], replicated, may hold values from -0.2 to 0.2
- cross: float32 [1], replicated, may hold values from -0.1 to 0.1
Outputs:
- updated: float32 [8, 2048, 8192], P(None, 'gx', 'gy')
- jump_rows: float32 [8, 2048, 8192], P(None, 'gx', 'gy')
- jump_cols: float32 [8, 2048, 8192], P(None, 'gx', 'gy')
The draws below stay inside these ranges and needn't reach their ends.
All inputs are finite; a program needn't handle non-finite values.
Results may differ from the reference program's by a relative error of at most 0.00005.
Values sent between devices are 32-bit elements; how exact they have to be, the bound alone decides.
No kernel may reach another device: no remote copies, remote signals or barrier semaphores. Data moves between devices by JAX's collectives and lax.ppermute only.
A program may use at most 128 MiB of HBM per device.

```python
import jax
import jax.numpy as jnp
from jax import lax

PLANES = 8
TAPS = 511
NR = 2048
NC = 8192


def shard_levels(key, extent, split, low, largest):
    def one(axis_at, blocks):
        heights = jax.random.uniform(jax.random.fold_in(jax.random.fold_in(key, 6), axis_at), (blocks,), jnp.float32, low / len(split), largest / len(split))
        return jnp.repeat(jnp.exp(heights), extent[axis_at] // blocks).reshape((-1,) + (1,) * (len(extent) - axis_at - 1))

    level = one(*split[0])
    for cut in split[1:]:
        level = level * one(*cut)
    return level


def normal_values(rng, shape, width, bound, shards=(), kind=jnp.bfloat16):
    values = jax.random.normal(rng, shape, jnp.float32) * width
    if len(shards) > 0:
        values = shard_levels(rng, shape, shards, -0.22, 0.18) * values
    return jnp.clip(values, min=-bound, max=bound).astype(kind)


def setup_inputs(seed: int = 0) -> dict:
    key_list = jax.random.split(jax.random.key(seed), 8)
    value = normal_values(key_list[0], (PLANES, NR, NC), 1.0, 6.0, ((1, 32), (2, 8)), jnp.float32)
    kernel_rows = jnp.clip(jax.random.uniform(key_list[1], (TAPS,), jnp.float32, 0.0009784736, 0.0029354207), 0.0009784736, 0.0029354207)
    kernel_cols = jnp.clip(jax.random.uniform(key_list[2], (TAPS,), jnp.float32, 0.0009784736, 0.0029354207), 0.0009784736, 0.0029354207)
    intensity = jnp.clip(jax.random.uniform(key_list[3], (2,), jnp.float32, 0.02, 0.1), 0.02, 0.1)
    diffusion = jnp.clip(jax.random.uniform(key_list[4], (3,), jnp.float32, 0.02, 0.1), 0.02, 0.1)
    drift = jnp.clip(jax.random.uniform(key_list[5], (3,), jnp.float32, -0.2, 0.2), -0.2, 0.2)
    cross = jnp.clip(jax.random.uniform(key_list[6], (1,), jnp.float32, -0.1, 0.1), -0.1, 0.1)
    return {"value": value, "kernel_rows": kernel_rows, "kernel_cols": kernel_cols, "intensity": intensity, "diffusion": diffusion, "drift": drift, "cross": cross}


def toeplitz(weights, out_len):
    span = out_len + weights.shape[0] - 1
    extended = jnp.concatenate([weights, jnp.zeros((span - weights.shape[0] + 1,), weights.dtype)])
    flattened = jnp.tile(extended, out_len)[: out_len * span]
    return flattened.reshape(out_len, span)


def banded(padded, weights, radius, along):
    length = padded.shape[along] - 2 * radius
    block_len = min(512, length)
    block_count = length // block_len
    matrix = toeplitz(weights, block_len)
    pattern = "pac,ba->pbc" if along == 1 else "pra,ba->prb"

    def one_block(block_id):
        window = lax.dynamic_slice_in_dim(padded, block_id * block_len, block_len + 2 * radius, along)
        return jnp.einsum(pattern, window, matrix, precision=lax.Precision.HIGHEST)

    stacked = lax.map(one_block, jnp.arange(block_count, dtype=jnp.int32))
    if along == 1:
        return jnp.transpose(stacked, (1, 0, 2, 3)).reshape(stacked.shape[1], length, stacked.shape[3])
    return jnp.transpose(stacked, (1, 2, 0, 3)).reshape(stacked.shape[1], stacked.shape[2], length)


def stencil(framed, diffusion, drift, cross):
    center = framed[1:-1, 1:-1, 1:-1]
    pairs = [
        (framed[1:-1, 2:, 1:-1], framed[1:-1, :-2, 1:-1]),
        (framed[1:-1, 1:-1, 2:], framed[1:-1, 1:-1, :-2]),
        (framed[2:, 1:-1, 1:-1], framed[:-2, 1:-1, 1:-1]),
    ]
    total = jnp.zeros_like(center)
    for axis_id in range(3):
        higher, lower = pairs[axis_id]
        total = total + diffusion[axis_id] * (higher - 2.0 * center + lower)
        total = total + drift[axis_id] * (higher - lower) * 0.5
    mixed = framed[1:-1, 2:, 2:] - framed[1:-1, 2:, :-2] - framed[1:-1, :-2, 2:] + framed[1:-1, :-2, :-2]
    return total + cross[0] * mixed * 0.25


def reference(value, kernel_rows, kernel_cols, intensity, diffusion, drift, cross):
    radius = (kernel_rows.shape[0] - 1) // 2
    padded_cols = jnp.pad(value, ((0, 0), (0, 0), (radius, radius)))
    jump_cols = banded(padded_cols, kernel_cols, radius, 2) - jnp.sum(kernel_cols) * value
    padded_rows = jnp.pad(value, ((0, 0), (radius, radius), (0, 0)))
    jump_rows = banded(padded_rows, kernel_rows, radius, 1) - jnp.sum(kernel_rows) * value
    framed = jnp.pad(value, 1)
    updated = value + stencil(framed, diffusion, drift, cross) + intensity[0] * jump_rows + intensity[1] * jump_cols
    return (updated, jump_rows, jump_cols)
```

```python
import jax
import jax.numpy as jnp
from jax import lax
from jax.experimental import pallas as pl
from jax.experimental.pallas import tpu as pltpu
from jax.sharding import PartitionSpec as P

BLOCK = 256
WINDOW = 3 * BLOCK
VMEM_LIMIT = 48 * 1024 * 1024


def split(x):
    high = x.astype(jnp.bfloat16)
    return high, (x - high.astype(jnp.float32)).astype(jnp.bfloat16)


def band(weights_ref):
    wide = jnp.broadcast_to(weights_ref[...], (BLOCK, WINDOW))
    return split(pltpu.roll(wide, 1, 1, stride=1, stride_axis=0))


def product(a, b, contract):
    dims = (contract, ((), ()))
    return (
        lax.dot_general(a[0], b[0], dims, preferred_element_type=jnp.float32)
        + lax.dot_general(a[0], b[1], dims, preferred_element_type=jnp.float32)
        + lax.dot_general(a[1], b[0], dims, preferred_element_type=jnp.float32)
    )


def local_kernel(coef, value, low, high, above, below, weights, jump_ref, part_ref, wide_hi, wide_lo):
    planes, rows, cols = value.shape
    for source, start in ((low, 0), (value, BLOCK), (high, BLOCK + cols)):
        hi, lo = split(source[...].reshape(planes * rows, source.shape[2]))
        wide_hi[:, start : start + source.shape[2]] = hi
        wide_lo[:, start : start + source.shape[2]] = lo
    taps = band(weights)
    total = coef[0]
    for start in range(0, cols, BLOCK):
        window = pl.ds(start, WINDOW)
        sums = product((wide_hi[:, window], wide_lo[:, window]), taps, ((1,), (1,)))
        jump_ref[:, :, start : start + BLOCK] = (
            sums.reshape(planes, rows, BLOCK) - total * value[:, :, start : start + BLOCK]
        )
    intensity = coef[1]
    row_diff, row_drift = coef[2], coef[5] * 0.5
    col_diff, col_drift = coef[3], coef[6] * 0.5
    plane_diff, plane_drift = coef[4], coef[7] * 0.5
    mixed = coef[8] * 0.25
    lane = lax.broadcasted_iota(jnp.int32, (rows, cols), 1)
    line = lax.broadcasted_iota(jnp.int32, (rows, cols), 0)
    side = lane.shape[1] - 1

    def along(x, first, last):
        right = jnp.where(lane[: x.shape[0]] == side, last, pltpu.roll(x, side, 1))
        left = jnp.where(lane[: x.shape[0]] == 0, first, pltpu.roll(x, 1, 1))
        return right, left

    edges = []
    for edge in (above, below):
        middle = edge[:, 128 : 128 + cols]
        lanes8 = lax.broadcasted_iota(jnp.int32, middle.shape, 1)
        right = jnp.where(lanes8 == side, edge[:, 128 + cols : 129 + cols], pltpu.roll(middle, side, 1))
        left = jnp.where(lanes8 == 0, edge[:, 127:128], pltpu.roll(middle, 1, 1))
        edges.append((middle, right - left))
    above_term = (row_diff - row_drift) * edges[0][0] - mixed * edges[0][1]
    below_term = (row_diff + row_drift) * edges[1][0] + mixed * edges[1][1]
    for p in range(planes):
        x = value[p]
        right, left = along(x, low[p, :, BLOCK - 1 : BLOCK], high[p, :, 0:1])
        slope = right - left
        out = x + col_diff * (right - 2.0 * x + left) + col_drift * slope
        down = (row_diff + row_drift) * x + mixed * slope
        up = (row_diff - row_drift) * x - mixed * slope
        down = jnp.where(line == rows - 1, below_term[p : p + 1], pltpu.roll(down, rows - 1, 0))
        up = jnp.where(line == 0, above_term[p : p + 1], pltpu.roll(up, 1, 0))
        out = out + (down - 2.0 * row_diff * x + up)
        out = out - 2.0 * plane_diff * x
        if p + 1 < planes:
            out = out + (plane_diff + plane_drift) * value[p + 1]
        if p > 0:
            out = out + (plane_diff - plane_drift) * value[p - 1]
        part_ref[p] = out + intensity * jump_ref[p]


def local_part(coef, value, low, high, above, below, weights):
    planes, rows, cols = value.shape
    vmem = pl.BlockSpec(memory_space=pltpu.VMEM)
    shape = jax.ShapeDtypeStruct(value.shape, jnp.float32)
    wide = pltpu.VMEM((planes * rows, cols + 2 * BLOCK), jnp.bfloat16)
    return pl.pallas_call(
        local_kernel,
        out_shape=(shape, shape),
        in_specs=[pl.BlockSpec(memory_space=pltpu.SMEM)] + [vmem] * 6,
        out_specs=(vmem, vmem),
        scratch_shapes=[wide, wide],
        compiler_params=pltpu.CompilerParams(vmem_limit_bytes=VMEM_LIMIT),
        cost_estimate=pl.CostEstimate(
            flops=6 * planes * rows * cols * WINDOW, bytes_accessed=16 * planes * rows * cols, transcendentals=0
        ),
        name="columns_and_stencil",
    )(coef, value, low, high, above, below, weights)


def rows_kernel(coef, column, weights, out_ref, tall_hi, tall_lo):
    rows, cols = column.shape
    zeros = jnp.zeros((BLOCK, cols), jnp.bfloat16)
    for tall in (tall_hi, tall_lo):
        tall[:BLOCK] = zeros
        tall[BLOCK + rows :] = zeros
    hi, lo = split(column[...])
    tall_hi[BLOCK : BLOCK + rows] = hi
    tall_lo[BLOCK : BLOCK + rows] = lo
    taps = band(weights)
    for start in range(0, rows, BLOCK):
        window = pl.ds(start, WINDOW)
        sums = product(taps, (tall_hi[window], tall_lo[window]), ((1,), (0,)))
        out_ref[start : start + BLOCK] = sums - coef[0] * column[start : start + BLOCK]


def rows_part(coef, column, weights):
    rows, cols = column.shape
    vmem = pl.BlockSpec(memory_space=pltpu.VMEM)
    tall = pltpu.VMEM((rows + 2 * BLOCK, cols), jnp.bfloat16)
    return pl.pallas_call(
        rows_kernel,
        out_shape=jax.ShapeDtypeStruct(column.shape, jnp.float32),
        in_specs=[pl.BlockSpec(memory_space=pltpu.SMEM), vmem, vmem],
        out_specs=vmem,
        scratch_shapes=[tall, tall],
        compiler_params=pltpu.CompilerParams(vmem_limit_bytes=VMEM_LIMIT),
        cost_estimate=pl.CostEstimate(
            flops=6 * rows * cols * WINDOW, bytes_accessed=8 * rows * cols, transcendentals=0
        ),
        name="rows",
    )(coef, column, weights)


def neighbours(low_side, high_side, axis):
    count = lax.axis_size(axis)
    forward = [(i, i + 1) for i in range(count - 1)]
    backward = [(i + 1, i) for i in range(count - 1)]
    return lax.ppermute(high_side, axis, forward), lax.ppermute(low_side, axis, backward)


def shards(value, kernel_rows, kernel_cols, intensity, diffusion, drift, cross):
    planes, rows, cols = value.shape
    devices = lax.axis_size("gx")
    groups = devices // planes
    width = cols // groups
    wide_rows = jnp.pad(kernel_rows, (0, WINDOW - kernel_rows.shape[0]))[None]
    wide_cols = jnp.pad(kernel_cols, (0, WINDOW - kernel_cols.shape[0]))[None]
    coef = jnp.concatenate([jnp.sum(kernel_cols)[None], intensity[1:2], diffusion, drift, cross])
    row_coef = jnp.sum(kernel_rows)[None]

    pieces = value.reshape(planes, rows, groups, width).transpose(0, 2, 1, 3)
    pieces = pieces.reshape(devices, rows, width)
    column = lax.all_to_all(pieces, "gx", 0, 0, tiled=True).reshape(devices * rows, width)

    low, high = neighbours(value[:, :, :BLOCK], value[:, :, cols - BLOCK :], "gy")

    def line(i):
        return jnp.concatenate([low[:, i, BLOCK - 128 :], value[:, i], high[:, i, :128]], axis=1)

    above, below = neighbours(line(0), line(rows - 1), "gx")
    jump_cols, part = local_part(coef, value, low, high, above, below, wide_cols)

    jump = rows_part(row_coef, column, wide_rows).reshape(devices, rows, width)
    back = lax.all_to_all(jump, "gx", 0, 0, tiled=True)
    jump_rows = back.reshape(planes, groups, rows, width).transpose(0, 2, 1, 3)
    jump_rows = jump_rows.reshape(planes, rows, cols)
    return part + intensity[0] * jump_rows, jump_rows, jump_cols


def solution(mesh):
    return jax.shard_map(
        shards,
        mesh=mesh,
        in_specs=(P(None, "gx", "gy"), P(), P(), P(), P(), P(), P()),
        out_specs=(P(None, "gx", "gy"), P(None, "gx", "gy"), P(None, "gx", "gy")),
        check_vma=False,
    )
```

```python
import jax
import jax.numpy as jnp
from jax import lax
from jax.experimental import pallas as pl
from jax.experimental.pallas import tpu as pltpu
from jax.sharding import PartitionSpec as P

BLOCK = 256
WINDOW = 3 * BLOCK
HALF = BLOCK // 2
EDGE = 128
RING = 4
CORES = 2
VMEM = pl.BlockSpec(memory_space=pltpu.VMEM)
SMEM = pl.BlockSpec(memory_space=pltpu.SMEM)


def params(mib):
    return pltpu.CompilerParams(vmem_limit_bytes=mib * 1024 * 1024)


def f32(*shape):
    return jax.ShapeDtypeStruct(shape, jnp.float32)


def split(x):
    high = x.astype(jnp.bfloat16)
    return high, (x - high.astype(jnp.float32)).astype(jnp.bfloat16)


def band(weights, wide):
    wide[...] = jnp.zeros_like(wide)
    wide[:, : weights.shape[1]] = weights[...]
    spread = jnp.broadcast_to(wide[...], (BLOCK, WINDOW))
    return split(pltpu.roll(spread, 1, 1, stride=1, stride_axis=0)), jnp.sum(wide[...], axis=1, keepdims=True)


def product(a, b, contract):
    dims = (contract, ((), ()))
    return (
        lax.dot_general(a[0], b[0], dims, preferred_element_type=jnp.float32)
        + lax.dot_general(a[0], b[1], dims, preferred_element_type=jnp.float32)
        + lax.dot_general(a[1], b[0], dims, preferred_element_type=jnp.float32)
    )


def ring(y, step):
    return lax.rem(y + (step + RING), RING)


def part_of(index, size):
    return pl.ds(pl.multiple_of(index * size, size), size)


def within_kernel(value, weights, out, taps_hi, taps_lo, total_ref, wide_hi, wide_lo, wide):
    planes, rows, cols = value.shape
    taps, total = band(weights, wide)
    taps_hi[...], taps_lo[...] = taps
    total_ref[...] = jnp.broadcast_to(total, total_ref.shape)
    wide_hi[...], wide_lo[...] = split(value[...].reshape(planes * rows, cols))
    for start in range(0, cols, BLOCK):
        first, last = max(0, start - BLOCK), min(cols, start + 2 * BLOCK)
        used = slice(first - start + BLOCK, last - start + BLOCK)
        sums = product(
            (wide_hi[:, first:last], wide_lo[:, first:last]), tuple(t[:, used] for t in taps), ((1,), (1,))
        )
        out[:, :, start : start + BLOCK] = (
            sums.reshape(planes, rows, BLOCK) - total[None] * value[:, :, start : start + BLOCK]
        )


def within_part(value, weights):
    planes, rows, cols = value.shape
    scratch = pltpu.VMEM((planes * rows, cols), jnp.bfloat16)
    taps = jax.ShapeDtypeStruct((BLOCK, WINDOW), jnp.bfloat16)
    return pl.pallas_call(
        within_kernel, out_shape=(f32(*value.shape), taps, taps, f32(8, EDGE)), in_specs=[VMEM] * 2,
        out_specs=[VMEM] * 4,
        scratch_shapes=[scratch, scratch, pltpu.VMEM((1, WINDOW), jnp.float32)], compiler_params=params(9), name="own_columns",
    )(value, weights)


def local_kernel(
    intensity, diffusion, drift, cross, value, low, high, above, below, within, taps_hi, taps_lo, jump_ref, part_ref
):
    planes, rows, cols = value.shape
    jump_ref[...] = within[...]
    for source, start, used in ((low, 0, slice(0, BLOCK)), (high, cols - BLOCK, slice(2 * BLOCK, WINDOW))):
        side = split(source[:, :rows].reshape(planes * rows, BLOCK))
        sums = product(side, (taps_hi[:, used], taps_lo[:, used]), ((1,), (1,)))
        jump_ref[:, :, start : start + BLOCK] += sums.reshape(planes, rows, BLOCK)
    row_diff, row_drift = diffusion[0], drift[0] * 0.5
    col_diff, col_drift = diffusion[1], drift[1] * 0.5
    plane_diff, plane_drift = diffusion[2], drift[2] * 0.5
    mixed = cross[0] * 0.25
    side = cols - 1

    def along(x, first, last):
        lane = lax.broadcasted_iota(jnp.int32, x.shape, 1)
        right = jnp.where(lane == side, last, pltpu.roll(x, side, 1))
        left = jnp.where(lane == 0, first, pltpu.roll(x, 1, 1))
        return right, left

    line = lax.broadcasted_iota(jnp.int32, (rows, cols), 0)
    for p in range(planes):
        edges = []
        for edge, row in ((above, rows), (below, rows + 1)):
            middle = edge[p : p + 1]
            right, left = along(middle, low[p, row : row + 1, BLOCK - 1 :], high[p, row : row + 1, :1])
            edges.append((middle, right - left))
        above_term = (row_diff - row_drift) * edges[0][0] - mixed * edges[0][1]
        below_term = (row_diff + row_drift) * edges[1][0] + mixed * edges[1][1]
        x = value[p]
        right, left = along(x, low[p, :rows, BLOCK - 1 :], high[p, :rows, :1])
        slope = right - left
        out = x + col_diff * (right - 2.0 * x + left) + col_drift * slope
        down = (row_diff + row_drift) * x + mixed * slope
        up = (row_diff - row_drift) * x - mixed * slope
        down = jnp.where(line == rows - 1, below_term, pltpu.roll(down, rows - 1, 0))
        up = jnp.where(line == 0, above_term, pltpu.roll(up, 1, 0))
        out = out + (down - 2.0 * row_diff * x + up)
        out = out - 2.0 * plane_diff * x
        if p + 1 < planes:
            out = out + (plane_diff + plane_drift) * value[p + 1]
        if p > 0:
            out = out + (plane_diff - plane_drift) * value[p - 1]
        part_ref[p] = out + intensity[1] * jump_ref[p]


def local_part(intensity, diffusion, drift, cross, value, low, high, above, below, within, taps):
    planes, rows, cols = value.shape
    return pl.pallas_call(
        local_kernel, out_shape=(f32(*value.shape),) * 2, in_specs=[SMEM] * 4 + [VMEM] * 8, out_specs=(VMEM, VMEM),
        compiler_params=params(6),
        name="side_columns_and_stencil",
    )(intensity, diffusion, drift, cross, value, low, high, above, below, within, *taps)


def tails_kernel(place, value, other, edge, high_side, low_side, above, below):
    planes, rows, cols = value.shape
    for core in range(CORES):

        @pl.when(place[2] == core)
        def _():
            for p in range(planes):
                line = slice(p, p + 1)
                above[line] = other[p, rows - 1 :, :] if core else edge[line]
                below[line] = edge[line] if core else other[p, :1, :]

    for out, start in ((high_side, cols - BLOCK), (low_side, 0)):
        columns = slice(start, start + BLOCK)
        out[:, :rows] = value[:, :, columns]
        for p in range(planes):
            out[p, rows : rows + 1] = above[p : p + 1, columns]
            out[p, rows + 1 : rows + 2] = below[p : p + 1, columns]
            out[p, rows + 2 :] = jnp.zeros((out.shape[1] - rows - 2, BLOCK), jnp.float32)


def tails_part(place, value, other, edge):
    planes, rows, cols = value.shape
    side = f32(planes, rows + 8, BLOCK)
    return pl.pallas_call(
        tails_kernel, out_shape=[side, side, f32(planes, cols), f32(planes, cols)], in_specs=[SMEM] + [VMEM] * 3,
        out_specs=[VMEM] * 4, compiler_params=params(4),
        name="tails",
    )(place, value, other, edge)


def taps_kernel(weights, high_ref, low_ref, total_ref, wide):
    (high_ref[...], low_ref[...]), total = band(weights, wide)
    total_ref[...] = jnp.broadcast_to(total, total_ref.shape)


def taps_part(weights):
    shape = jax.ShapeDtypeStruct((BLOCK, WINDOW), jnp.bfloat16)
    return pl.pallas_call(
        taps_kernel, out_shape=(shape, shape, f32(8, EDGE)), in_specs=[VMEM], out_specs=(VMEM,) * 3,
        scratch_shapes=[pltpu.VMEM((1, WINDOW), jnp.float32)], compiler_params=params(8), name="row_taps",
    )(weights)


def load_kernel(place, value, held, line, done):
    copy = pltpu.make_async_copy(value, held, done)
    copy.start()
    copy.wait()
    planes, rows, _ = value.shape
    for core, row in ((0, 0), (1, rows - 1)):

        @pl.when(place[2] == core)
        def _():
            for p in range(planes):
                line[p : p + 1] = held[p, row : row + 1, :]


def load_part(place, value):
    planes, _, cols = value.shape
    return pl.pallas_call(
        load_kernel, out_shape=[f32(*value.shape), f32(planes, cols)],
        in_specs=[SMEM, pl.BlockSpec(memory_space=pl.ANY)], out_specs=[VMEM] * 2,
        scratch_shapes=[pltpu.SemaphoreType.DMA], compiler_params=params(4), name="load",
    )(place, value)


def pieces_kernel(steps, place, value, other, *refs):
    outs, done = refs[:-1], refs[-1]
    y, core = place[1], place[2]
    rows = value.shape[1]
    copies = []
    for i, (k, out) in enumerate(zip(steps, outs)):
        plane = CORES * ring(y, k) + core
        for j, (source, at) in enumerate(((value, core), (other, 1 - core))):
            copies.append(pltpu.make_async_copy(source.at[plane], out.at[part_of(at, rows)], done.at[i, j]))
    for copy in copies:
        copy.start()
    for copy in copies:
        copy.wait()


def pieces_part(steps, place, value, other):
    _, rows, cols = value.shape
    anywhere = pl.BlockSpec(memory_space=pl.ANY)
    return pl.pallas_call(
        lambda *refs: pieces_kernel(steps, *refs),
        out_shape=[f32(CORES * rows, cols)] * len(steps), in_specs=[SMEM, anywhere, anywhere],
        out_specs=[VMEM] * len(steps), scratch_shapes=[pltpu.SemaphoreType.DMA((len(steps), 2))],
        compiler_params=params(4), name="pieces",
    )(place, value, other)


def tap_tile(taps, at, size):
    return tuple(t[:, at : at + size] for t in taps)


def near_kernel(place, p0, p1, p3, taps_hi, taps_lo, total, out, hold):
    y = place[1]
    taps = (taps_hi, taps_lo)
    size = p0.shape[0]
    for k, piece in ((0, p0), (1, p1), (3, p3)):
        hold[part_of(ring(y, -k), size)] = piece[...]
    hold[part_of(ring(y, -2), size)] = jnp.zeros_like(p0)
    first, second = split(hold[:BLOCK]), split(hold[BLOCK:])
    dims = ((1,), (0,))
    scale = total[0:1, 0:1]
    out[:BLOCK] = (
        product(tap_tile(taps, BLOCK, BLOCK), first, dims)
        + product(tap_tile(taps, 2 * BLOCK, BLOCK), second, dims)
        - scale * hold[:BLOCK]
    )
    out[BLOCK:] = (
        product(tap_tile(taps, 0, BLOCK), first, dims)
        + product(tap_tile(taps, BLOCK, BLOCK), second, dims)
        - scale * hold[BLOCK:]
    )


def near_part(place, p0, p1, p3, taps):
    size, cols = p0.shape
    return pl.pallas_call(
        near_kernel, out_shape=f32(RING * size, cols), in_specs=[SMEM] + [VMEM] * 6, out_specs=VMEM,
        scratch_shapes=[pltpu.VMEM((RING * size, cols), jnp.float32)], compiler_params=params(9), name="near_rows",
    )(place, p0, p1, p3, *taps)


def middle_kernel(place, near, p2, x0, x1, x3, taps_hi, taps_lo, total, out, opposite, hold):
    y = place[1]
    taps = (taps_hi, taps_lo)
    size = p2.shape[0]
    at = ring(y, -2)
    dims = ((1,), (0,))
    for k, piece in ((0, x0), (1, x1), (3, x3)):
        hold[part_of(ring(y, -k), size)] = piece[...]
    hold[part_of(at, size)] = jnp.zeros_like(p2)
    rows2 = split(p2[...])
    below, above = split(hold[:BLOCK]), split(hold[BLOCK:])
    for i, far, tile in ((0, above, 0), (1, below, 2 * BLOCK)):
        column = part_of(at + 2 - 2 * i, HALF)
        mine = tuple(t[:, column] for t in taps)
        out[i * BLOCK : (i + 1) * BLOCK] = (
            near[i * BLOCK : (i + 1) * BLOCK]
            + product(mine, rows2, dims)
            + product(tap_tile(taps, tile, BLOCK), far, dims)
        )
    mid = out[part_of(at, size)] - total[0:1, 0:1] * p2[...]
    out[part_of(at, size)] = mid
    opposite[...] = mid


def middle_part(place, near, p2, x0, x1, x3, taps):
    rows, cols = near.shape
    size = rows // RING
    return pl.pallas_call(
        middle_kernel, out_shape=(f32(rows, cols), f32(size, cols)), in_specs=[SMEM] + [VMEM] * 8,
        out_specs=(VMEM, VMEM), scratch_shapes=[pltpu.VMEM((rows, cols), jnp.float32)],
        compiler_params=params(9),
        name="middle_rows",
    )(place, near, p2, x0, x1, x3, *taps)


def last_kernel(place, middle, x2, taps_hi, taps_lo, b0, b1, b3, hold):
    y = place[1]
    taps = (taps_hi, taps_lo)
    size = x2.shape[0]
    at = ring(y, -2)
    dims = ((1,), (0,))
    hold[...] = middle[...]
    far = split(x2[...])

    @pl.when(at >= RING // 2)
    def _():
        column = part_of(at - RING // 2, HALF)
        hold[:BLOCK] += product(tuple(t[:, column] for t in taps), far, dims)

    @pl.when(at < RING // 2)
    def _():
        column = part_of(at + RING, HALF)
        hold[BLOCK:] += product(tuple(t[:, column] for t in taps), far, dims)

    for k, out in ((0, b0), (1, b1), (3, b3)):
        out[...] = hold[part_of(ring(y, -k), size)]


def last_part(place, middle, x2, taps):
    rows, cols = middle.shape
    return pl.pallas_call(
        last_kernel, out_shape=[f32(rows // RING, cols)] * 3, in_specs=[SMEM] + [VMEM] * 4, out_specs=[VMEM] * 3,
        scratch_shapes=[pltpu.VMEM((rows, cols), jnp.float32)], compiler_params=params(9), name="last_rows",
    )(place, middle, x2, *taps[:2])


def swap_kernel(place, da, db, out):
    rows = out.shape[1]
    for k, source in enumerate((da, db)):
        out[k] = source[part_of(1 - place[2], rows)]


def swap_part(place, da, db):
    rows, cols = da.shape
    return pl.pallas_call(
        swap_kernel, out_shape=f32(2, rows // CORES, cols), in_specs=[SMEM] + [VMEM] * 2, out_specs=VMEM,
        compiler_params=params(8), name="swap",
    )(place, da, db)


def finish_kernel(steps, place, intensity, da, db, other, part, *refs):
    updated, jump, new_updated, new_jump, done = refs[-5:]
    y, core = place[1], place[2]
    rows = other.shape[1]
    copies = []
    for i, (step, source) in enumerate(zip(steps, (da, db))):
        for j in range(CORES):
            at = CORES * i + j
            plane = CORES * ring(y, step) + (1 - core if j else core)
            block = other[i] if j else source[part_of(core, rows)]
            new_jump[at] = block
            new_updated[at] = part[plane] + intensity[0] * block
            for k, (new, out) in enumerate(((new_jump, jump), (new_updated, updated))):
                copy = pltpu.make_async_copy(new.at[at], out.at[plane], done.at[at, k])
                copy.start()
                copies.append(copy)
    for copy in copies:
        copy.wait()


def finish_part(steps, place, intensity, da, db, other, part, results):
    planes, rows, cols = part.shape
    anywhere = pl.BlockSpec(memory_space=pl.ANY)
    scratch = pltpu.VMEM((2 * CORES, rows, cols), jnp.float32)
    return pl.pallas_call(
        lambda *refs: finish_kernel(steps, *refs),
        out_shape=[f32(*part.shape)] * 2, in_specs=[SMEM, SMEM] + [VMEM] * 4 + [anywhere] * len(results),
        out_specs=[anywhere] * 2, scratch_shapes=[scratch, scratch, pltpu.SemaphoreType.DMA((2 * CORES, 2))],
        input_output_aliases={6: 0, 7: 1} if results else {},
        compiler_params=params(8), name="finish",
    )(place, intensity, da, db, other, part, *results)


def neighbours(low_side, high_side, axis):
    count = lax.axis_size(axis)
    forward = [(i, i + 1) for i in range(count - 1)]
    backward = [(i + 1, i) for i in range(count - 1)]
    return lax.ppermute(high_side, axis, forward), lax.ppermute(low_side, axis, backward)


def send(block, move):
    route = []
    for i in range(RING * RING * CORES):
        x, y, core = move(i // (RING * CORES), i // CORES % RING, i % CORES)
        if 0 <= x < RING:
            route.append((i, (x * RING + y % RING) * CORES + core))
    return lax.ppermute(block, "gx", route)


def to_ring(block, step):
    return send(block, lambda x, y, core: (x, y + step, core))


def to_other_core(block):
    return send(block, lambda x, y, core: (x, y, 1 - core))


def across_chips(line):
    ends = lax.axis_size("gx") - 1
    route = [(i, i + 1 if i % CORES else i - 1) for i in range(1, ends)]
    return lax.ppermute(line, "gx", route)


def to_group(block, k):
    return send(block, lambda x, y, core: (x + 1 if (y - k) % RING >= RING // 2 else x - 1, y, core))


def after(x, *others):
    return lax.optimization_barrier((x, *others))[0]


def shards(value, kernel_rows, kernel_cols, intensity, diffusion, drift, cross):
    planes, rows, cols = value.shape
    me = lax.axis_index("gx")
    chip = lax.div(me, CORES)
    place = jnp.stack([lax.div(chip, RING), lax.rem(chip, RING), lax.rem(me, CORES)])

    other = to_other_core(value)
    value, line = load_part(place, value)
    edge = across_chips(line)

    s1, s3, p0 = pieces_part((1, 3, 0), place, value, other)
    p1, p3, x0 = to_ring(s1, 1), to_ring(s3, 3), to_group(p0, 0)
    (s2,) = pieces_part((2,), after(place, p0, edge), value, other)
    within, col_hi, col_lo, _ = within_part(value, after(kernel_cols[None], s2))
    taps = taps_part(after(kernel_rows[None], within))
    p2 = to_ring(after(s2, p1, p3, taps[2]), 2)
    x1, x3 = to_group(after(p1, x0), 1), to_group(after(p3, x0), 3)
    high_side, low_side, above, below = tails_part(after(place, p0), value, other, edge)
    low, high = neighbours(low_side, high_side, "gy")
    near = near_part(after(place, low, high), p0, p1, p3, taps)
    x2 = to_group(p2, 2)
    middle, b2 = middle_part(place, near, p2, x0, x1, x3, taps)
    d2 = to_ring(b2, -2)
    jump_cols, part = local_part(
        after(intensity, b2), diffusion, drift, cross, value, low, high, above, below, within, (col_hi, col_lo)
    )
    b0, b1, b3 = last_part(after(place, part), middle, x2, taps)
    d1, d3 = to_ring(b1, -1), to_ring(b3, -3)
    swapped = to_other_core(swap_part(place, b0, d2))
    results = finish_part((0, 2), place, intensity, b0, d2, swapped, part, ())
    swapped = to_other_core(swap_part(place, d1, d3))
    updated, jump_rows = finish_part((1, 3), place, intensity, d1, d3, swapped, part, results)
    return updated, jump_rows, jump_cols


def solution(mesh):
    return jax.shard_map(
        shards,
        mesh=mesh,
        in_specs=(P(None, "gx", "gy"), P(), P(), P(), P(), P(), P()),
        out_specs=(P(None, "gx", "gy"), P(None, "gx", "gy"), P(None, "gx", "gy")),
        check_vma=False,
    )
```

```python
import jax
import jax.numpy as jnp
from jax import lax
from jax.experimental import pallas as pl
from jax.experimental.pallas import tpu as pltpu
from jax.sharding import PartitionSpec as P

BLOCK = 256
WINDOW = 3 * BLOCK
HALF = BLOCK // 2
EDGE = 128
RING = 4
CORES = 2
VMEM = pl.BlockSpec(memory_space=pltpu.VMEM)
SMEM = pl.BlockSpec(memory_space=pltpu.SMEM)


def params(mib):
    return pltpu.CompilerParams(vmem_limit_bytes=mib * 1024 * 1024)


def f32(*shape):
    return jax.ShapeDtypeStruct(shape, jnp.float32)


def split(x):
    high = x.astype(jnp.bfloat16)
    return high, (x - high.astype(jnp.float32)).astype(jnp.bfloat16)


def band(weights, wide):
    wide[...] = jnp.zeros_like(wide)
    wide[:, : weights.shape[1]] = weights[...]
    spread = jnp.broadcast_to(wide[...], (BLOCK, WINDOW))
    return split(pltpu.roll(spread, 1, 1, stride=1, stride_axis=0)), jnp.sum(wide[...], axis=1, keepdims=True)


def product(a, b, contract):
    dims = (contract, ((), ()))
    return (
        lax.dot_general(a[0], b[0], dims, preferred_element_type=jnp.float32)
        + lax.dot_general(a[0], b[1], dims, preferred_element_type=jnp.float32)
        + lax.dot_general(a[1], b[0], dims, preferred_element_type=jnp.float32)
    )


def ring(y, step):
    return lax.rem(y + (step + RING), RING)


def part_of(index, size):
    return pl.ds(pl.multiple_of(index * size, size), size)


def within_kernel(value, weights, out, taps_hi, taps_lo, total_ref, wide_hi, wide_lo, wide):
    planes, rows, cols = value.shape
    taps, total = band(weights, wide)
    taps_hi[...], taps_lo[...] = taps
    total_ref[...] = jnp.broadcast_to(total, total_ref.shape)
    wide_hi[...], wide_lo[...] = split(value[...].reshape(planes * rows, cols))
    for start in range(0, cols, BLOCK):
        first, last = max(0, start - BLOCK), min(cols, start + 2 * BLOCK)
        used = slice(first - start + BLOCK, last - start + BLOCK)
        sums = product(
            (wide_hi[:, first:last], wide_lo[:, first:last]), tuple(t[:, used] for t in taps), ((1,), (1,))
        )
        out[:, :, start : start + BLOCK] = (
            sums.reshape(planes, rows, BLOCK) - total[None] * value[:, :, start : start + BLOCK]
        )


def within_part(value, weights):
    planes, rows, cols = value.shape
    scratch = pltpu.VMEM((planes * rows, cols), jnp.bfloat16)
    taps = jax.ShapeDtypeStruct((BLOCK, WINDOW), jnp.bfloat16)
    return pl.pallas_call(
        within_kernel, out_shape=(f32(*value.shape), taps, taps, f32(8, EDGE)), in_specs=[VMEM] * 2,
        out_specs=[VMEM] * 4,
        scratch_shapes=[scratch, scratch, pltpu.VMEM((1, WINDOW), jnp.float32)], compiler_params=params(9), name="own_columns",
    )(value, weights)


def local_kernel(
    place, intensity, diffusion, drift, cross, value, low, high, beside, edge, within, taps_hi, taps_lo,
    jump_ref, part_ref, frame,
):
    planes, rows, cols = value.shape
    jump_ref[...] = within[...]
    for source, start, used in ((low, 0, slice(0, BLOCK)), (high, cols - BLOCK, slice(2 * BLOCK, WINDOW))):
        side = split(source[:, :rows].reshape(planes * rows, BLOCK))
        sums = product(side, (taps_hi[:, used], taps_lo[:, used]), ((1,), (1,)))
        jump_ref[:, :, start : start + BLOCK] += sums.reshape(planes, rows, BLOCK)
    row_diff, row_drift = diffusion[0], drift[0] * 0.5
    col_diff, col_drift = diffusion[1], drift[1] * 0.5
    plane_diff, plane_drift = diffusion[2], drift[2] * 0.5
    mixed = cross[0] * 0.25
    side = cols - 1

    def along(x, first, last):
        lane = lax.broadcasted_iota(jnp.int32, x.shape, 1)
        right = jnp.where(lane == side, last, pltpu.roll(x, side, 1))
        left = jnp.where(lane == 0, first, pltpu.roll(x, 1, 1))
        return right, left

    core = place[2]
    frame[core] = edge[...]
    frame[1 - core] = beside[...]
    edges = []
    for i in range(2):
        middle = frame[i, :, EDGE : EDGE + cols]
        right, left = along(middle, frame[i, :, EDGE - 1 : EDGE], frame[i, :, EDGE + cols : EDGE + cols + 1])
        edges.append((middle, right - left))
    above_terms = (row_diff - row_drift) * edges[0][0] - mixed * edges[0][1]
    below_terms = (row_diff + row_drift) * edges[1][0] + mixed * edges[1][1]
    line = lax.broadcasted_iota(jnp.int32, (rows, cols), 0)
    for p in range(planes):
        above_term, below_term = above_terms[p : p + 1], below_terms[p : p + 1]
        x = value[p]
        right, left = along(x, low[p, :rows, BLOCK - 1 :], high[p, :rows, :1])
        slope = right - left
        out = x + col_diff * (right - 2.0 * x + left) + col_drift * slope
        down = (row_diff + row_drift) * x + mixed * slope
        up = (row_diff - row_drift) * x - mixed * slope
        down = jnp.where(line == rows - 1, below_term, pltpu.roll(down, rows - 1, 0))
        up = jnp.where(line == 0, above_term, pltpu.roll(up, 1, 0))
        out = out + (down - 2.0 * row_diff * x + up)
        out = out - 2.0 * plane_diff * x
        if p + 1 < planes:
            out = out + (plane_diff + plane_drift) * value[p + 1]
        if p > 0:
            out = out + (plane_diff - plane_drift) * value[p - 1]
        part_ref[p] = out + intensity[1] * jump_ref[p]


def local_part(place, intensity, diffusion, drift, cross, value, low, high, beside, edge, within, taps):
    planes, rows, cols = value.shape
    return pl.pallas_call(
        local_kernel, out_shape=(f32(*value.shape),) * 2, in_specs=[SMEM] * 5 + [VMEM] * 8, out_specs=(VMEM, VMEM),
        scratch_shapes=[pltpu.VMEM((2, planes, cols + 2 * EDGE), jnp.float32)],
        compiler_params=params(6), name="side_columns_and_stencil",
    )(place, intensity, diffusion, drift, cross, value, low, high, beside, edge, within, *taps)


def lines_kernel(place, value, low, high, outer, inner):
    planes, rows, cols = value.shape
    for core in range(CORES):

        @pl.when(place[2] == core)
        def _():
            for out, row in ((outer, (rows - 1) * core), (inner, (rows - 1) * (1 - core))):
                for p in range(planes):
                    out[p : p + 1, :EDGE] = low[p, row : row + 1, BLOCK - EDGE :]
                    out[p : p + 1, EDGE : EDGE + cols] = value[p, row : row + 1, :]
                    out[p : p + 1, EDGE + cols :] = high[p, row : row + 1, :EDGE]


def lines_part(place, value, low, high):
    planes, _, cols = value.shape
    return pl.pallas_call(
        lines_kernel, out_shape=[f32(planes, cols + 2 * EDGE)] * 2, in_specs=[SMEM] + [VMEM] * 3,
        out_specs=[VMEM] * 2, compiler_params=params(4), name="lines",
    )(place, value, low, high)


def taps_kernel(weights, high_ref, low_ref, total_ref, wide):
    (high_ref[...], low_ref[...]), total = band(weights, wide)
    total_ref[...] = jnp.broadcast_to(total, total_ref.shape)


def taps_part(weights):
    shape = jax.ShapeDtypeStruct((BLOCK, WINDOW), jnp.bfloat16)
    return pl.pallas_call(
        taps_kernel, out_shape=(shape, shape, f32(8, EDGE)), in_specs=[VMEM], out_specs=(VMEM,) * 3,
        scratch_shapes=[pltpu.VMEM((1, WINDOW), jnp.float32)], compiler_params=params(8), name="row_taps",
    )(weights)


def load_kernel(value, held, high_side, low_side, done):
    copy = pltpu.make_async_copy(value, held, done)
    copy.start()
    copy.wait()
    cols = value.shape[2]
    high_side[...] = held[:, :, cols - BLOCK :]
    low_side[...] = held[:, :, :BLOCK]


def load_part(value):
    side = f32(*value.shape[:2], BLOCK)
    return pl.pallas_call(
        load_kernel, out_shape=[f32(*value.shape), side, side], in_specs=[pl.BlockSpec(memory_space=pl.ANY)],
        out_specs=[VMEM] * 3, scratch_shapes=[pltpu.SemaphoreType.DMA], compiler_params=params(4), name="load",
    )(value)


def pieces_kernel(steps, place, value, other, *refs):
    outs, done = refs[:-1], refs[-1]
    y, core = place[1], place[2]
    rows = value.shape[1]
    copies = []
    for i, (k, out) in enumerate(zip(steps, outs)):
        plane = CORES * ring(y, k) + core
        for j, (source, at) in enumerate(((value, core), (other, 1 - core))):
            copies.append(pltpu.make_async_copy(source.at[plane], out.at[part_of(at, rows)], done.at[i, j]))
    for copy in copies:
        copy.start()
    for copy in copies:
        copy.wait()


def pieces_part(steps, place, value, other):
    _, rows, cols = value.shape
    anywhere = pl.BlockSpec(memory_space=pl.ANY)
    return pl.pallas_call(
        lambda *refs: pieces_kernel(steps, *refs),
        out_shape=[f32(CORES * rows, cols)] * len(steps), in_specs=[SMEM, anywhere, anywhere],
        out_specs=[VMEM] * len(steps), scratch_shapes=[pltpu.SemaphoreType.DMA((len(steps), 2))],
        compiler_params=params(4), name="pieces",
    )(place, value, other)


def tap_tile(taps, at, size):
    return tuple(t[:, at : at + size] for t in taps)


def near_kernel(place, p0, p1, p3, taps_hi, taps_lo, total, out, hold):
    y = place[1]
    taps = (taps_hi, taps_lo)
    size = p0.shape[0]
    for k, piece in ((0, p0), (1, p1), (3, p3)):
        hold[part_of(ring(y, -k), size)] = piece[...]
    hold[part_of(ring(y, -2), size)] = jnp.zeros_like(p0)
    first, second = split(hold[:BLOCK]), split(hold[BLOCK:])
    dims = ((1,), (0,))
    scale = total[0:1, 0:1]
    out[:BLOCK] = (
        product(tap_tile(taps, BLOCK, BLOCK), first, dims)
        + product(tap_tile(taps, 2 * BLOCK, BLOCK), second, dims)
        - scale * hold[:BLOCK]
    )
    out[BLOCK:] = (
        product(tap_tile(taps, 0, BLOCK), first, dims)
        + product(tap_tile(taps, BLOCK, BLOCK), second, dims)
        - scale * hold[BLOCK:]
    )


def near_part(place, p0, p1, p3, taps):
    size, cols = p0.shape
    return pl.pallas_call(
        near_kernel, out_shape=f32(RING * size, cols), in_specs=[SMEM] + [VMEM] * 6, out_specs=VMEM,
        scratch_shapes=[pltpu.VMEM((RING * size, cols), jnp.float32)], compiler_params=params(9), name="near_rows",
    )(place, p0, p1, p3, *taps)


def gather_halo(y, pieces, hold):
    for k, piece in pieces:
        hold[part_of(ring(y, -k), piece.shape[0])] = piece[...]


def opposite_kernel(place, near, p2, x0, x1, x3, taps_hi, taps_lo, total, same, other, hold):
    y, core = place[1], place[2]
    size, rows = p2.shape[0], same.shape[0]
    at = ring(y, -2)
    gather_halo(y, ((0, x0), (1, x1), (3, x3)), hold)
    hold[part_of(at, size)] = jnp.zeros_like(p2)
    pair, half = lax.div(at, 2), lax.rem(at, 2)
    lines = part_of(half, HALF)
    near_taps = tuple(t[lines, part_of(2 + half, HALF)] for t in (taps_hi, taps_lo))
    far_taps = tuple(t[lines, part_of(2 * pair, BLOCK)] for t in (taps_hi, taps_lo))
    dims = ((1,), (0,))
    out = (
        near[part_of(at, size)]
        + product(near_taps, split(p2[...]), dims)
        + product(far_taps, split(hold[part_of(1 - pair, BLOCK)]), dims)
        - total[0:1, 0:1] * p2[...]
    )
    hold[:size] = out
    same[...] = hold[part_of(core, rows)]
    other[...] = hold[part_of(1 - core, rows)]


def opposite_part(place, near, p2, x0, x1, x3, taps):
    rows, cols = near.shape
    return pl.pallas_call(
        opposite_kernel, out_shape=[f32(rows // RING // CORES, cols)] * 2, in_specs=[SMEM] + [VMEM] * 8,
        out_specs=[VMEM] * 2, scratch_shapes=[pltpu.VMEM((rows, cols), jnp.float32)], compiler_params=params(9),
        name="opposite_rows",
    )(place, near, p2, x0, x1, x3, *taps)


def others_kernel(
    place, near, p2, x0, x1, x2, x3, taps_hi, taps_lo, same0, other0, same1, other1, same3, other3, hold, total
):
    y, core = place[1], place[2]
    taps = (taps_hi, taps_lo)
    size, rows = p2.shape[0], same0.shape[0]
    at = ring(y, -2)
    dims = ((1,), (0,))
    gather_halo(y, ((0, x0), (1, x1), (2, x2), (3, x3)), hold)
    rows2 = split(p2[...])
    below, above = split(hold[:BLOCK]), split(hold[BLOCK:])
    for i, far, tile in ((0, above, 0), (1, below, 2 * BLOCK)):
        column = part_of(at + 2 - 2 * i, HALF)
        total[i * BLOCK : (i + 1) * BLOCK] = (
            near[i * BLOCK : (i + 1) * BLOCK]
            + product(tuple(t[:, column] for t in taps), rows2, dims)
            + product(tap_tile(taps, tile, BLOCK), far, dims)
        )
    for k, same, other in ((0, same0, other0), (1, same1, other1), (3, same3, other3)):
        first = CORES * ring(y, -k)
        same[...] = total[part_of(first + core, rows)]
        other[...] = total[part_of(first + 1 - core, rows)]


def others_part(place, near, p2, x0, x1, x2, x3, taps):
    rows, cols = near.shape
    scratch = pltpu.VMEM((rows, cols), jnp.float32)
    return pl.pallas_call(
        others_kernel, out_shape=[f32(rows // RING // CORES, cols)] * 6, in_specs=[SMEM] + [VMEM] * 8,
        out_specs=[VMEM] * 6, scratch_shapes=[scratch, scratch], compiler_params=params(10), name="other_rows",
    )(place, near, p2, x0, x1, x2, x3, *taps[:2])


def finish_kernel(steps, place, intensity, same1, other1, same2, other2, part, *refs):
    updated, jump, new_updated, new_jump, done = refs[-5:]
    y, core = place[1], place[2]
    copies = []
    for i, (step, blocks) in enumerate(zip(steps, ((same1, other1), (same2, other2)))):
        for j, block in enumerate(blocks):
            at = CORES * i + j
            plane = CORES * ring(y, step) + (1 - core if j else core)
            new_jump[at] = block[...]
            new_updated[at] = part[plane] + intensity[0] * block[...]
            for k, (new, out) in enumerate(((new_jump, jump), (new_updated, updated))):
                copy = pltpu.make_async_copy(new.at[at], out.at[plane], done.at[at, k])
                copy.start()
                copies.append(copy)
    for copy in copies:
        copy.wait()


def finish_part(steps, place, intensity, blocks, part, results):
    planes, rows, cols = part.shape
    anywhere = pl.BlockSpec(memory_space=pl.ANY)
    scratch = pltpu.VMEM((2 * CORES, rows, cols), jnp.float32)
    return pl.pallas_call(
        lambda *refs: finish_kernel(steps, *refs),
        out_shape=[f32(*part.shape)] * 2, in_specs=[SMEM, SMEM] + [VMEM] * 5 + [anywhere] * len(results),
        out_specs=[anywhere] * 2, scratch_shapes=[scratch, scratch, pltpu.SemaphoreType.DMA((2 * CORES, 2))],
        input_output_aliases={7: 0, 8: 1} if results else {},
        compiler_params=params(8), name="finish",
    )(place, intensity, *blocks, part, *results)


def neighbours(low_side, high_side, axis):
    count = lax.axis_size(axis)
    forward = [(i, i + 1) for i in range(count - 1)]
    backward = [(i + 1, i) for i in range(count - 1)]
    return lax.ppermute(high_side, axis, forward), lax.ppermute(low_side, axis, backward)


def send(block, move):
    route = []
    for i in range(RING * RING * CORES):
        x, y, core = move(i // (RING * CORES), i // CORES % RING, i % CORES)
        if 0 <= x < RING:
            route.append((i, (x * RING + y % RING) * CORES + core))
    return lax.ppermute(block, "gx", route)


def to_ring(block, step, flip=False):
    return send(block, lambda x, y, core: (x, y + step, 1 - core if flip else core))


def to_other_core(block):
    return send(block, lambda x, y, core: (x, y, 1 - core))


def across_chips(line):
    ends = lax.axis_size("gx") - 1
    route = [(i, i + 1 if i % CORES else i - 1) for i in range(1, ends)]
    return lax.ppermute(line, "gx", route)


def to_group(block, k):
    return send(block, lambda x, y, core: (x + 1 if (y - k) % RING >= RING // 2 else x - 1, y, core))


def after(x, *others):
    return lax.optimization_barrier((x, *others))[0]


def shards(value, kernel_rows, kernel_cols, intensity, diffusion, drift, cross):
    planes, rows, cols = value.shape
    me = lax.axis_index("gx")
    chip = lax.div(me, CORES)
    place = jnp.stack([lax.div(chip, RING), lax.rem(chip, RING), lax.rem(me, CORES)])

    other = to_other_core(value)
    value, high_side, low_side = load_part(value)

    s1, s3, p0, s2 = pieces_part((1, 3, 0, 2), place, value, other)
    p1, p3, x0 = to_ring(s1, 1), to_ring(s3, 3), to_group(p0, 0)
    low, high = neighbours(after(low_side, p0), after(high_side, p0), "gy")
    within, col_hi, col_lo, _ = within_part(value, after(kernel_cols[None], s2))
    taps = taps_part(after(kernel_rows[None], within))
    p2 = to_ring(after(s2, p1, p3, taps[2]), 2)
    x1, x3 = to_group(after(p1, low, high), 1), to_group(after(p3, x0), 3)
    outer, inner = lines_part(after(place, p1), value, low, high)
    edge, beside = across_chips(outer), to_other_core(inner)
    near = near_part(after(place, outer), p0, p1, p3, taps)
    x2 = to_group(after(p2, near), 2)
    b2, o2 = opposite_part(place, near, p2, x0, x1, x3, taps)
    d2, o2 = to_ring(b2, -2), to_ring(o2, -2, True)
    b0, o0, b1, o1, b3, o3 = others_part(place, near, p2, x0, x1, x2, x3, taps)
    d1, d3 = to_ring(b1, -1), to_ring(b3, -3)
    o1, o3 = to_ring(o1, -1, True), to_ring(o3, -3, True)
    o0 = to_other_core(o0)
    jump_cols, part = local_part(
        place, after(intensity, b0), diffusion, drift, cross, value, low, high, beside, edge, within, (col_hi, col_lo)
    )
    results = finish_part((0, 2), place, intensity, (b0, o0, d2, o2), part, ())
    updated, jump_rows = finish_part((1, 3), place, intensity, (d1, o1, d3, o3), part, results)
    return updated, jump_rows, jump_cols


def solution(mesh):
    return jax.shard_map(
        shards,
        mesh=mesh,
        in_specs=(P(None, "gx", "gy"), P(), P(), P(), P(), P(), P()),
        out_specs=(P(None, "gx", "gy"), P(None, "gx", "gy"), P(None, "gx", "gy")),
        check_vma=False,
    )
```

```python
import jax
import jax.numpy as jnp
from jax import lax
from jax.experimental import pallas as pl
from jax.experimental.pallas import tpu as pltpu
from jax.sharding import PartitionSpec as P

BLOCK = 256
WINDOW = 3 * BLOCK
HALF = BLOCK // 2
EDGE = 128
RING = 4
CORES = 2
VMEM = pl.BlockSpec(memory_space=pltpu.VMEM)
SMEM = pl.BlockSpec(memory_space=pltpu.SMEM)


def params(mib):
    return pltpu.CompilerParams(vmem_limit_bytes=mib * 1024 * 1024)


def f32(*shape):
    return jax.ShapeDtypeStruct(shape, jnp.float32)


def split(x):
    high = x.astype(jnp.bfloat16)
    return high, (x - high.astype(jnp.float32)).astype(jnp.bfloat16)


def band(weights, wide):
    wide[...] = jnp.zeros_like(wide)
    wide[:, : weights.shape[1]] = weights[...]
    spread = jnp.broadcast_to(wide[...], (BLOCK, WINDOW))
    return split(pltpu.roll(spread, 1, 1, stride=1, stride_axis=0)), jnp.sum(wide[...], axis=1, keepdims=True)


def product(a, b, contract):
    dims = (contract, ((), ()))
    return (
        lax.dot_general(a[0], b[0], dims, preferred_element_type=jnp.float32)
        + lax.dot_general(a[0], b[1], dims, preferred_element_type=jnp.float32)
        + lax.dot_general(a[1], b[0], dims, preferred_element_type=jnp.float32)
    )


def ring(y, step):
    return lax.rem(y + (step + RING), RING)


def part_of(index, size):
    return pl.ds(pl.multiple_of(index * size, size), size)


def within_kernel(value, weights, out, taps_hi, taps_lo, total_ref, wide_hi, wide_lo, wide):
    planes, rows, cols = value.shape
    taps, total = band(weights, wide)
    taps_hi[...], taps_lo[...] = taps
    total_ref[...] = jnp.broadcast_to(total, total_ref.shape)
    wide_hi[...], wide_lo[...] = split(value[...].reshape(planes * rows, cols))
    for start in range(0, cols, BLOCK):
        first, last = max(0, start - BLOCK), min(cols, start + 2 * BLOCK)
        used = slice(first - start + BLOCK, last - start + BLOCK)
        sums = product(
            (wide_hi[:, first:last], wide_lo[:, first:last]), tuple(t[:, used] for t in taps), ((1,), (1,))
        )
        out[:, :, start : start + BLOCK] = (
            sums.reshape(planes, rows, BLOCK) - total[None] * value[:, :, start : start + BLOCK]
        )


def within_part(value, weights):
    planes, rows, cols = value.shape
    scratch = pltpu.VMEM((planes * rows, cols), jnp.bfloat16)
    taps = jax.ShapeDtypeStruct((BLOCK, WINDOW), jnp.bfloat16)
    return pl.pallas_call(
        within_kernel, out_shape=(f32(*value.shape), taps, taps, f32(8, EDGE)), in_specs=[VMEM] * 2,
        out_specs=[VMEM] * 4,
        scratch_shapes=[scratch, scratch, pltpu.VMEM((1, WINDOW), jnp.float32)], compiler_params=params(9), name="own_columns",
    )(value, weights)


def local_kernel(
    place, intensity, diffusion, drift, cross, value, low, high, beside, edge, within, taps_hi, taps_lo,
    jump_ref, part_ref, frame,
):
    planes, rows, cols = value.shape
    jump_ref[...] = within[...]
    for source, start, used in ((low, 0, slice(0, BLOCK)), (high, cols - BLOCK, slice(2 * BLOCK, WINDOW))):
        side = split(source[:, :rows].reshape(planes * rows, BLOCK))
        sums = product(side, (taps_hi[:, used], taps_lo[:, used]), ((1,), (1,)))
        jump_ref[:, :, start : start + BLOCK] += sums.reshape(planes, rows, BLOCK)
    row_diff, row_drift = diffusion[0], drift[0] * 0.5
    col_diff, col_drift = diffusion[1], drift[1] * 0.5
    plane_diff, plane_drift = diffusion[2], drift[2] * 0.5
    mixed = cross[0] * 0.25
    side = cols - 1

    def along(x, first, last):
        lane = lax.broadcasted_iota(jnp.int32, x.shape, 1)
        right = jnp.where(lane == side, last, pltpu.roll(x, side, 1))
        left = jnp.where(lane == 0, first, pltpu.roll(x, 1, 1))
        return right, left

    core = place[2]
    frame[core] = edge[...]
    frame[1 - core] = beside[...]
    edges = []
    for i in range(2):
        middle = frame[i, :, EDGE : EDGE + cols]
        right, left = along(middle, frame[i, :, EDGE - 1 : EDGE], frame[i, :, EDGE + cols : EDGE + cols + 1])
        edges.append((middle, right - left))
    above_terms = (row_diff - row_drift) * edges[0][0] - mixed * edges[0][1]
    below_terms = (row_diff + row_drift) * edges[1][0] + mixed * edges[1][1]
    line = lax.broadcasted_iota(jnp.int32, (rows, cols), 0)
    for p in range(planes):
        above_term, below_term = above_terms[p : p + 1], below_terms[p : p + 1]
        x = value[p]
        right, left = along(x, low[p, :rows, BLOCK - 1 :], high[p, :rows, :1])
        slope = right - left
        out = x + col_diff * (right - 2.0 * x + left) + col_drift * slope
        down = (row_diff + row_drift) * x + mixed * slope
        up = (row_diff - row_drift) * x - mixed * slope
        down = jnp.where(line == rows - 1, below_term, pltpu.roll(down, rows - 1, 0))
        up = jnp.where(line == 0, above_term, pltpu.roll(up, 1, 0))
        out = out + (down - 2.0 * row_diff * x + up)
        out = out - 2.0 * plane_diff * x
        if p + 1 < planes:
            out = out + (plane_diff + plane_drift) * value[p + 1]
        if p > 0:
            out = out + (plane_diff - plane_drift) * value[p - 1]
        part_ref[p] = out + intensity[1] * jump_ref[p]


def local_part(place, intensity, diffusion, drift, cross, value, low, high, beside, edge, within, taps):
    planes, rows, cols = value.shape
    return pl.pallas_call(
        local_kernel, out_shape=(f32(*value.shape),) * 2, in_specs=[SMEM] * 5 + [VMEM] * 8, out_specs=(VMEM, VMEM),
        scratch_shapes=[pltpu.VMEM((2, planes, cols + 2 * EDGE), jnp.float32)],
        compiler_params=params(6), name="side_columns_and_stencil",
    )(place, intensity, diffusion, drift, cross, value, low, high, beside, edge, within, *taps)


def lines_kernel(place, value, low, high, outer, inner):
    planes, rows, cols = value.shape
    for core in range(CORES):

        @pl.when(place[2] == core)
        def _():
            for out, row in ((outer, (rows - 1) * core), (inner, (rows - 1) * (1 - core))):
                for p in range(planes):
                    out[p : p + 1, :EDGE] = low[p, row : row + 1, BLOCK - EDGE :]
                    out[p : p + 1, EDGE : EDGE + cols] = value[p, row : row + 1, :]
                    out[p : p + 1, EDGE + cols :] = high[p, row : row + 1, :EDGE]


def lines_part(place, value, low, high):
    planes, _, cols = value.shape
    return pl.pallas_call(
        lines_kernel, out_shape=[f32(planes, cols + 2 * EDGE)] * 2, in_specs=[SMEM] + [VMEM] * 3,
        out_specs=[VMEM] * 2, compiler_params=params(4), name="lines",
    )(place, value, low, high)


def taps_kernel(weights, high_ref, low_ref, total_ref, wide):
    (high_ref[...], low_ref[...]), total = band(weights, wide)
    total_ref[...] = jnp.broadcast_to(total, total_ref.shape)


def taps_part(weights):
    shape = jax.ShapeDtypeStruct((BLOCK, WINDOW), jnp.bfloat16)
    return pl.pallas_call(
        taps_kernel, out_shape=(shape, shape, f32(8, EDGE)), in_specs=[VMEM], out_specs=(VMEM,) * 3,
        scratch_shapes=[pltpu.VMEM((1, WINDOW), jnp.float32)], compiler_params=params(8), name="row_taps",
    )(weights)


def load_kernel(place, value, held, high_side, low_side, done):
    copy = pltpu.make_async_copy(value, held, done)
    copy.start()
    copy.wait()
    cols = value.shape[2]
    high_side[...] = held[:, :, cols - BLOCK :]
    low_side[...] = held[:, :, :BLOCK]


def load_part(place, value):
    side = f32(*value.shape[:2], BLOCK)
    return pl.pallas_call(
        load_kernel, out_shape=[f32(*value.shape), side, side], in_specs=[SMEM, pl.BlockSpec(memory_space=pl.ANY)],
        out_specs=[VMEM] * 3, scratch_shapes=[pltpu.SemaphoreType.DMA], compiler_params=params(4), name="load",
    )(place, value)


def pieces_kernel(steps, place, value, other, *refs):
    outs, done = refs[:-1], refs[-1]
    y, core = place[1], place[2]
    rows = value.shape[1]
    copies = []
    for i, (k, out) in enumerate(zip(steps, outs)):
        plane = CORES * ring(y, k) + core
        for j, (source, at) in enumerate(((value, core), (other, 1 - core))):
            copies.append(pltpu.make_async_copy(source.at[plane], out.at[part_of(at, rows)], done.at[i, j]))
    for copy in copies:
        copy.start()
    for copy in copies:
        copy.wait()


def pieces_part(steps, place, value, other):
    _, rows, cols = value.shape
    return pl.pallas_call(
        lambda *refs: pieces_kernel(steps, *refs),
        out_shape=[f32(CORES * rows, cols)] * len(steps), in_specs=[SMEM, VMEM, VMEM],
        out_specs=[VMEM] * len(steps), scratch_shapes=[pltpu.SemaphoreType.DMA((len(steps), 2))],
        compiler_params=params(4), name="pieces",
    )(place, value, other)


def tap_tile(taps, at, size):
    return tuple(t[:, at : at + size] for t in taps)


def near_kernel(place, p0, p1, p3, taps_hi, taps_lo, total, out, hold):
    y = place[1]
    taps = (taps_hi, taps_lo)
    size = p0.shape[0]
    for k, piece in ((0, p0), (1, p1), (3, p3)):
        hold[part_of(ring(y, -k), size)] = piece[...]
    hold[part_of(ring(y, -2), size)] = jnp.zeros_like(p0)
    first, second = split(hold[:BLOCK]), split(hold[BLOCK:])
    dims = ((1,), (0,))
    scale = total[0:1, 0:1]
    out[:BLOCK] = (
        product(tap_tile(taps, BLOCK, BLOCK), first, dims)
        + product(tap_tile(taps, 2 * BLOCK, BLOCK), second, dims)
        - scale * hold[:BLOCK]
    )
    out[BLOCK:] = (
        product(tap_tile(taps, 0, BLOCK), first, dims)
        + product(tap_tile(taps, BLOCK, BLOCK), second, dims)
        - scale * hold[BLOCK:]
    )


def near_part(place, p0, p1, p3, taps):
    size, cols = p0.shape
    return pl.pallas_call(
        near_kernel, out_shape=f32(RING * size, cols), in_specs=[SMEM] + [VMEM] * 6, out_specs=VMEM,
        scratch_shapes=[pltpu.VMEM((RING * size, cols), jnp.float32)], compiler_params=params(9), name="near_rows",
    )(place, p0, p1, p3, *taps)


def gather_halo(y, pieces, hold):
    for k, piece in pieces:
        hold[part_of(ring(y, -k), piece.shape[0])] = piece[...]


def opposite_kernel(place, near, p2, x0, x1, x3, taps_hi, taps_lo, total, same, other, hold):
    y, core = place[1], place[2]
    size, rows = p2.shape[0], same.shape[0]
    at = ring(y, -2)
    gather_halo(y, ((0, x0), (1, x1), (3, x3)), hold)
    hold[part_of(at, size)] = jnp.zeros_like(p2)
    pair, half = lax.div(at, 2), lax.rem(at, 2)
    lines = part_of(half, HALF)
    near_taps = tuple(t[lines, part_of(2 + half, HALF)] for t in (taps_hi, taps_lo))
    far_taps = tuple(t[lines, part_of(2 * pair, BLOCK)] for t in (taps_hi, taps_lo))
    dims = ((1,), (0,))
    out = (
        near[part_of(at, size)]
        + product(near_taps, split(p2[...]), dims)
        + product(far_taps, split(hold[part_of(1 - pair, BLOCK)]), dims)
        - total[0:1, 0:1] * p2[...]
    )
    hold[:size] = out
    same[...] = hold[part_of(core, rows)]
    other[...] = hold[part_of(1 - core, rows)]


def opposite_part(place, near, p2, x0, x1, x3, taps):
    rows, cols = near.shape
    return pl.pallas_call(
        opposite_kernel, out_shape=[f32(rows // RING // CORES, cols)] * 2, in_specs=[SMEM] + [VMEM] * 8,
        out_specs=[VMEM] * 2, scratch_shapes=[pltpu.VMEM((rows, cols), jnp.float32)], compiler_params=params(9),
        name="opposite_rows",
    )(place, near, p2, x0, x1, x3, *taps)


def others_kernel(
    place, near, p2, x0, x1, x2, x3, taps_hi, taps_lo, same0, other0, same1, other1, same3, other3, hold, total
):
    y, core = place[1], place[2]
    taps = (taps_hi, taps_lo)
    size, rows = p2.shape[0], same0.shape[0]
    at = ring(y, -2)
    dims = ((1,), (0,))
    gather_halo(y, ((0, x0), (1, x1), (2, x2), (3, x3)), hold)
    rows2 = split(p2[...])
    below, above = split(hold[:BLOCK]), split(hold[BLOCK:])
    for i, far, tile in ((0, above, 0), (1, below, 2 * BLOCK)):
        column = part_of(at + 2 - 2 * i, HALF)
        total[i * BLOCK : (i + 1) * BLOCK] = (
            near[i * BLOCK : (i + 1) * BLOCK]
            + product(tuple(t[:, column] for t in taps), rows2, dims)
            + product(tap_tile(taps, tile, BLOCK), far, dims)
        )
    for k, same, other in ((0, same0, other0), (1, same1, other1), (3, same3, other3)):
        first = CORES * ring(y, -k)
        same[...] = total[part_of(first + core, rows)]
        other[...] = total[part_of(first + 1 - core, rows)]


def others_part(place, near, p2, x0, x1, x2, x3, taps):
    rows, cols = near.shape
    scratch = pltpu.VMEM((rows, cols), jnp.float32)
    return pl.pallas_call(
        others_kernel, out_shape=[f32(rows // RING // CORES, cols)] * 6, in_specs=[SMEM] + [VMEM] * 8,
        out_specs=[VMEM] * 6, scratch_shapes=[scratch, scratch], compiler_params=params(10), name="other_rows",
    )(place, near, p2, x0, x1, x2, x3, *taps[:2])


def finish_kernel(steps, place, intensity, same1, other1, same2, other2, part, *refs):
    updated, jump, new_updated, new_jump, done = refs[-5:]
    y, core = place[1], place[2]
    copies = []
    for i, (step, blocks) in enumerate(zip(steps, ((same1, other1), (same2, other2)))):
        for j, block in enumerate(blocks):
            at = CORES * i + j
            plane = CORES * ring(y, step) + (1 - core if j else core)
            new_jump[at] = block[...]
            new_updated[at] = part[plane] + intensity[0] * block[...]
            for k, (new, out) in enumerate(((new_jump, jump), (new_updated, updated))):
                copy = pltpu.make_async_copy(new.at[at], out.at[plane], done.at[at, k])
                copy.start()
                copies.append(copy)
    for copy in copies:
        copy.wait()


def finish_part(steps, place, intensity, blocks, part, results):
    planes, rows, cols = part.shape
    anywhere = pl.BlockSpec(memory_space=pl.ANY)
    scratch = pltpu.VMEM((2 * CORES, rows, cols), jnp.float32)
    return pl.pallas_call(
        lambda *refs: finish_kernel(steps, *refs),
        out_shape=[f32(*part.shape)] * 2, in_specs=[SMEM, SMEM] + [VMEM] * 5 + [anywhere] * len(results),
        out_specs=[anywhere] * 2, scratch_shapes=[scratch, scratch, pltpu.SemaphoreType.DMA((2 * CORES, 2))],
        input_output_aliases={7: 0, 8: 1} if results else {},
        compiler_params=params(8), name="finish",
    )(place, intensity, *blocks, part, *results)


def neighbours(low_side, high_side, axis):
    count = lax.axis_size(axis)
    forward = [(i, i + 1) for i in range(count - 1)]
    backward = [(i + 1, i) for i in range(count - 1)]
    return lax.ppermute(high_side, axis, forward), lax.ppermute(low_side, axis, backward)


def send(block, move):
    route = []
    for i in range(RING * RING * CORES):
        x, y, core = move(i // (RING * CORES), i // CORES % RING, i % CORES)
        if 0 <= x < RING:
            route.append((i, (x * RING + y % RING) * CORES + core))
    return lax.ppermute(block, "gx", route)


def to_ring(block, step, flip=False):
    return send(block, lambda x, y, core: (x, y + step, 1 - core if flip else core))


def to_other_core(block):
    return send(block, lambda x, y, core: (x, y, 1 - core))


def across_chips(line):
    ends = lax.axis_size("gx") - 1
    route = [(i, i + 1 if i % CORES else i - 1) for i in range(1, ends)]
    return lax.ppermute(line, "gx", route)


def to_group(block, k):
    return send(block, lambda x, y, core: (x + 1 if (y - k) % RING >= RING // 2 else x - 1, y, core))


def after(x, *others):
    return lax.optimization_barrier((x, *others))[0]


def shards(value, kernel_rows, kernel_cols, intensity, diffusion, drift, cross):
    planes, rows, cols = value.shape
    me = lax.axis_index("gx")
    chip = lax.div(me, CORES)
    place = jnp.stack([lax.div(chip, RING), lax.rem(chip, RING), lax.rem(me, CORES)])

    other = to_other_core(value)
    value, high_side, low_side = load_part(place, value)

    s1, s3, p0, s2 = pieces_part((1, 3, 0, 2), place, value, other)
    p1, p3, x0 = to_ring(s1, 1), to_ring(s3, 3), to_group(p0, 0)
    low, high = neighbours(after(low_side, p0), after(high_side, p0), "gy")
    within, col_hi, col_lo, _ = within_part(value, after(kernel_cols[None], s2))
    taps = taps_part(after(kernel_rows[None], within))
    p2 = to_ring(after(s2, p1, p3, taps[2]), 2)
    x1, x3 = to_group(p1, 1), to_group(p3, 3)
    outer, inner = lines_part(after(place, p1), value, low, high)
    edge, beside = across_chips(outer), to_other_core(inner)
    near = near_part(after(place, outer, x0), p0, p1, p3, taps)
    x2 = to_group(after(p2, near), 2)
    b2, o2 = opposite_part(place, near, p2, x0, x1, x3, taps)
    d2, o2 = to_ring(b2, -2), to_ring(o2, -2, True)
    b0, o0, b1, o1, b3, o3 = others_part(place, near, p2, x0, x1, x2, x3, taps)
    d1, d3 = to_ring(b1, -1), to_ring(b3, -3)
    o1, o3 = to_ring(o1, -1, True), to_ring(o3, -3, True)
    o0 = to_other_core(o0)
    jump_cols, part = local_part(
        place, after(intensity, b0), diffusion, drift, cross, value, low, high, beside, edge, within, (col_hi, col_lo)
    )
    results = finish_part((0, 2), place, intensity, (b0, o0, d2, o2), part, ())
    updated, jump_rows = finish_part((1, 3), place, intensity, (d1, o1, d3, o3), part, results)
    return updated, jump_rows, jump_cols


def solution(mesh):
    return jax.shard_map(
        shards,
        mesh=mesh,
        in_specs=(P(None, "gx", "gy"), P(), P(), P(), P(), P(), P()),
        out_specs=(P(None, "gx", "gy"), P(None, "gx", "gy"), P(None, "gx", "gy")),
        check_vma=False,
    )
```

```python
import jax
import jax.numpy as jnp
from jax import lax
from jax.experimental import pallas as pl
from jax.experimental.pallas import tpu as pltpu
from jax.sharding import PartitionSpec as P

BLOCK = 256
WINDOW = 3 * BLOCK
HALF = BLOCK // 2
EDGE = 128
RING = 4
CORES = 2
VMEM = pl.BlockSpec(memory_space=pltpu.VMEM)
SMEM = pl.BlockSpec(memory_space=pltpu.SMEM)


def params(mib):
    return pltpu.CompilerParams(vmem_limit_bytes=mib * 1024 * 1024)


def f32(*shape):
    return jax.ShapeDtypeStruct(shape, jnp.float32)


def split(x):
    high = x.astype(jnp.bfloat16)
    return high, (x - high.astype(jnp.float32)).astype(jnp.bfloat16)


def band(weights, wide):
    wide[...] = jnp.zeros_like(wide)
    wide[:, : weights.shape[1]] = weights[...]
    spread = jnp.broadcast_to(wide[...], (BLOCK, WINDOW))
    return split(pltpu.roll(spread, 1, 1, stride=1, stride_axis=0)), jnp.sum(wide[...], axis=1, keepdims=True)


def product(a, b, contract):
    dims = (contract, ((), ()))
    return (
        lax.dot_general(a[0], b[0], dims, preferred_element_type=jnp.float32)
        + lax.dot_general(a[0], b[1], dims, preferred_element_type=jnp.float32)
        + lax.dot_general(a[1], b[0], dims, preferred_element_type=jnp.float32)
    )


def ring(y, step):
    return lax.rem(y + (step + RING), RING)


def part_of(index, size):
    return pl.ds(pl.multiple_of(index * size, size), size)


def within_kernel(value, weights, out, taps_hi, taps_lo, total_ref, wide_hi, wide_lo, wide):
    planes, rows, cols = value.shape
    taps, total = band(weights, wide)
    taps_hi[...], taps_lo[...] = taps
    total_ref[...] = jnp.broadcast_to(total, total_ref.shape)
    wide_hi[...], wide_lo[...] = split(value[...].reshape(planes * rows, cols))
    for start in range(0, cols, BLOCK):
        first, last = max(0, start - BLOCK), min(cols, start + 2 * BLOCK)
        used = slice(first - start + BLOCK, last - start + BLOCK)
        sums = product(
            (wide_hi[:, first:last], wide_lo[:, first:last]), tuple(t[:, used] for t in taps), ((1,), (1,))
        )
        out[:, :, start : start + BLOCK] = (
            sums.reshape(planes, rows, BLOCK) - total[None] * value[:, :, start : start + BLOCK]
        )


def within_part(value, weights):
    planes, rows, cols = value.shape
    scratch = pltpu.VMEM((planes * rows, cols), jnp.bfloat16)
    taps = jax.ShapeDtypeStruct((BLOCK, WINDOW), jnp.bfloat16)
    return pl.pallas_call(
        within_kernel, out_shape=(f32(*value.shape), taps, taps, f32(8, EDGE)), in_specs=[VMEM] * 2,
        out_specs=[VMEM] * 4,
        scratch_shapes=[scratch, scratch, pltpu.VMEM((1, WINDOW), jnp.float32)], compiler_params=params(9), name="own_columns",
    )(value, weights)


def local_kernel(
    place, intensity, diffusion, drift, cross, value, low, high, beside, edge, within, taps_hi, taps_lo,
    jump_ref, part_ref, frame,
):
    planes, rows, cols = value.shape
    jump_ref[...] = within[...]
    for source, start, used in ((low, 0, slice(0, BLOCK)), (high, cols - BLOCK, slice(2 * BLOCK, WINDOW))):
        side = split(source[:, :rows].reshape(planes * rows, BLOCK))
        sums = product(side, (taps_hi[:, used], taps_lo[:, used]), ((1,), (1,)))
        jump_ref[:, :, start : start + BLOCK] += sums.reshape(planes, rows, BLOCK)
    row_diff, row_drift = diffusion[0], drift[0] * 0.5
    col_diff, col_drift = diffusion[1], drift[1] * 0.5
    plane_diff, plane_drift = diffusion[2], drift[2] * 0.5
    mixed = cross[0] * 0.25
    side = cols - 1

    def along(x, first, last):
        lane = lax.broadcasted_iota(jnp.int32, x.shape, 1)
        right = jnp.where(lane == side, last, pltpu.roll(x, side, 1))
        left = jnp.where(lane == 0, first, pltpu.roll(x, 1, 1))
        return right, left

    core = place[2]
    frame[core] = edge[...]
    frame[1 - core] = beside[...]
    edges = []
    for i in range(2):
        middle = frame[i, :, EDGE : EDGE + cols]
        right, left = along(middle, frame[i, :, EDGE - 1 : EDGE], frame[i, :, EDGE + cols : EDGE + cols + 1])
        edges.append((middle, right - left))
    above_terms = (row_diff - row_drift) * edges[0][0] - mixed * edges[0][1]
    below_terms = (row_diff + row_drift) * edges[1][0] + mixed * edges[1][1]
    line = lax.broadcasted_iota(jnp.int32, (rows, cols), 0)
    for p in range(planes):
        above_term, below_term = above_terms[p : p + 1], below_terms[p : p + 1]
        x = value[p]
        right, left = along(x, low[p, :rows, BLOCK - 1 :], high[p, :rows, :1])
        slope = right - left
        out = x + col_diff * (right - 2.0 * x + left) + col_drift * slope
        down = (row_diff + row_drift) * x + mixed * slope
        up = (row_diff - row_drift) * x - mixed * slope
        down = jnp.where(line == rows - 1, below_term, pltpu.roll(down, rows - 1, 0))
        up = jnp.where(line == 0, above_term, pltpu.roll(up, 1, 0))
        out = out + (down - 2.0 * row_diff * x + up)
        out = out - 2.0 * plane_diff * x
        if p + 1 < planes:
            out = out + (plane_diff + plane_drift) * value[p + 1]
        if p > 0:
            out = out + (plane_diff - plane_drift) * value[p - 1]
        part_ref[p] = out + intensity[1] * jump_ref[p]


def local_part(place, intensity, diffusion, drift, cross, value, low, high, beside, edge, within, taps):
    planes, rows, cols = value.shape
    return pl.pallas_call(
        local_kernel, out_shape=(f32(*value.shape),) * 2, in_specs=[SMEM] * 5 + [VMEM] * 8, out_specs=(VMEM, VMEM),
        scratch_shapes=[pltpu.VMEM((2, planes, cols + 2 * EDGE), jnp.float32)],
        compiler_params=params(6), name="side_columns_and_stencil",
    )(place, intensity, diffusion, drift, cross, value, low, high, beside, edge, within, *taps)


def lines_kernel(place, value, low, high, outer, inner):
    planes, rows, cols = value.shape
    for core in range(CORES):

        @pl.when(place[2] == core)
        def _():
            for out, row in ((outer, (rows - 1) * core), (inner, (rows - 1) * (1 - core))):
                for p in range(planes):
                    out[p : p + 1, :EDGE] = low[p, row : row + 1, BLOCK - EDGE :]
                    out[p : p + 1, EDGE : EDGE + cols] = value[p, row : row + 1, :]
                    out[p : p + 1, EDGE + cols :] = high[p, row : row + 1, :EDGE]


def lines_part(place, value, low, high):
    planes, _, cols = value.shape
    return pl.pallas_call(
        lines_kernel, out_shape=[f32(planes, cols + 2 * EDGE)] * 2, in_specs=[SMEM] + [VMEM] * 3,
        out_specs=[VMEM] * 2, compiler_params=params(4), name="lines",
    )(place, value, low, high)


def taps_kernel(weights, high_ref, low_ref, total_ref, wide):
    (high_ref[...], low_ref[...]), total = band(weights, wide)
    total_ref[...] = jnp.broadcast_to(total, total_ref.shape)


def taps_part(weights):
    shape = jax.ShapeDtypeStruct((BLOCK, WINDOW), jnp.bfloat16)
    return pl.pallas_call(
        taps_kernel, out_shape=(shape, shape, f32(8, EDGE)), in_specs=[VMEM], out_specs=(VMEM,) * 3,
        scratch_shapes=[pltpu.VMEM((1, WINDOW), jnp.float32)], compiler_params=params(8), name="row_taps",
    )(weights)


def load_kernel(place, value, held, high_side, low_side, done):
    copy = pltpu.make_async_copy(value, held, done)
    copy.start()
    copy.wait()
    cols = value.shape[2]
    high_side[...] = held[:, :, cols - BLOCK :]
    low_side[...] = held[:, :, :BLOCK]


def load_part(place, value):
    side = f32(*value.shape[:2], BLOCK)
    return pl.pallas_call(
        load_kernel, out_shape=[f32(*value.shape), side, side], in_specs=[SMEM, pl.BlockSpec(memory_space=pl.ANY)],
        out_specs=[VMEM] * 3, scratch_shapes=[pltpu.SemaphoreType.DMA], compiler_params=params(4), name="load",
    )(place, value)


def pieces_kernel(steps, place, value, other, *refs):
    outs, done = refs[:-1], refs[-1]
    y, core = place[1], place[2]
    rows = value.shape[1]
    copies = []
    for i, (k, out) in enumerate(zip(steps, outs)):
        plane = CORES * ring(y, k) + core
        for j, (source, at) in enumerate(((value, core), (other, 1 - core))):
            copies.append(pltpu.make_async_copy(source.at[plane], out.at[part_of(at, rows)], done.at[i, j]))
    for copy in copies:
        copy.start()
    for copy in copies:
        copy.wait()


def pieces_part(steps, place, value, other):
    _, rows, cols = value.shape
    return pl.pallas_call(
        lambda *refs: pieces_kernel(steps, *refs),
        out_shape=[f32(CORES * rows, cols)] * len(steps), in_specs=[SMEM, VMEM, VMEM],
        out_specs=[VMEM] * len(steps), scratch_shapes=[pltpu.SemaphoreType.DMA((len(steps), 2))],
        compiler_params=params(4), name="pieces",
    )(place, value, other)


def tap_tile(taps, at, size):
    return tuple(t[:, at : at + size] for t in taps)


def near_kernel(place, p0, p1, p3, taps_hi, taps_lo, total, out, hold):
    y = place[1]
    taps = (taps_hi, taps_lo)
    size = p0.shape[0]
    for k, piece in ((0, p0), (1, p1), (3, p3)):
        hold[part_of(ring(y, -k), size)] = piece[...]
    hold[part_of(ring(y, -2), size)] = jnp.zeros_like(p0)
    first, second = split(hold[:BLOCK]), split(hold[BLOCK:])
    dims = ((1,), (0,))
    scale = total[0:1, 0:1]
    out[:BLOCK] = (
        product(tap_tile(taps, BLOCK, BLOCK), first, dims)
        + product(tap_tile(taps, 2 * BLOCK, BLOCK), second, dims)
        - scale * hold[:BLOCK]
    )
    out[BLOCK:] = (
        product(tap_tile(taps, 0, BLOCK), first, dims)
        + product(tap_tile(taps, BLOCK, BLOCK), second, dims)
        - scale * hold[BLOCK:]
    )


def near_part(place, p0, p1, p3, taps):
    size, cols = p0.shape
    return pl.pallas_call(
        near_kernel, out_shape=f32(RING * size, cols), in_specs=[SMEM] + [VMEM] * 6, out_specs=VMEM,
        scratch_shapes=[pltpu.VMEM((RING * size, cols), jnp.float32)], compiler_params=params(9), name="near_rows",
    )(place, p0, p1, p3, *taps)


def gather_halo(y, pieces, hold):
    for k, piece in pieces:
        hold[part_of(ring(y, -k), piece.shape[0])] = piece[...]


def opposite_kernel(place, near, p2, x0, x1, x3, taps_hi, taps_lo, total, same, other, hold):
    y, core = place[1], place[2]
    size, rows = p2.shape[0], same.shape[0]
    at = ring(y, -2)
    gather_halo(y, ((0, x0), (1, x1), (3, x3)), hold)
    hold[part_of(at, size)] = jnp.zeros_like(p2)
    pair, half = lax.div(at, 2), lax.rem(at, 2)
    lines = part_of(half, HALF)
    near_taps = tuple(t[lines, part_of(2 + half, HALF)] for t in (taps_hi, taps_lo))
    far_taps = tuple(t[lines, part_of(2 * pair, BLOCK)] for t in (taps_hi, taps_lo))
    dims = ((1,), (0,))
    out = (
        near[part_of(at, size)]
        + product(near_taps, split(p2[...]), dims)
        + product(far_taps, split(hold[part_of(1 - pair, BLOCK)]), dims)
        - total[0:1, 0:1] * p2[...]
    )
    hold[:size] = out
    same[...] = hold[part_of(core, rows)]
    other[...] = hold[part_of(1 - core, rows)]


def opposite_part(place, near, p2, x0, x1, x3, taps):
    rows, cols = near.shape
    return pl.pallas_call(
        opposite_kernel, out_shape=[f32(rows // RING // CORES, cols)] * 2, in_specs=[SMEM] + [VMEM] * 8,
        out_specs=[VMEM] * 2, scratch_shapes=[pltpu.VMEM((rows, cols), jnp.float32)], compiler_params=params(9),
        name="opposite_rows",
    )(place, near, p2, x0, x1, x3, *taps)


def others_kernel(
    place, near, p2, x0, x1, x2, x3, taps_hi, taps_lo, same0, other0, same1, other1, same3, other3, hold, total
):
    y, core = place[1], place[2]
    taps = (taps_hi, taps_lo)
    size, rows = p2.shape[0], same0.shape[0]
    at = ring(y, -2)
    dims = ((1,), (0,))
    gather_halo(y, ((0, x0), (1, x1), (2, x2), (3, x3)), hold)
    rows2 = split(p2[...])
    below, above = split(hold[:BLOCK]), split(hold[BLOCK:])
    for i, far, tile in ((0, above, 0), (1, below, 2 * BLOCK)):
        column = part_of(at + 2 - 2 * i, HALF)
        total[i * BLOCK : (i + 1) * BLOCK] = (
            near[i * BLOCK : (i + 1) * BLOCK]
            + product(tuple(t[:, column] for t in taps), rows2, dims)
            + product(tap_tile(taps, tile, BLOCK), far, dims)
        )
    for k, same, other in ((0, same0, other0), (1, same1, other1), (3, same3, other3)):
        first = CORES * ring(y, -k)
        same[...] = total[part_of(first + core, rows)]
        other[...] = total[part_of(first + 1 - core, rows)]


def others_part(place, near, p2, x0, x1, x2, x3, taps):
    rows, cols = near.shape
    scratch = pltpu.VMEM((rows, cols), jnp.float32)
    return pl.pallas_call(
        others_kernel, out_shape=[f32(rows // RING // CORES, cols)] * 6, in_specs=[SMEM] + [VMEM] * 8,
        out_specs=[VMEM] * 6, scratch_shapes=[scratch, scratch], compiler_params=params(10), name="other_rows",
    )(place, near, p2, x0, x1, x2, x3, *taps[:2])


def finish_kernel(steps, place, intensity, *refs):
    count = len(steps)
    blocks, part = refs[:count], refs[count]
    updated, jump, new_updated, new_jump, done = refs[-5:]
    y, core = place[1], place[2]
    copies = []
    for at, ((step, flip), block) in enumerate(zip(steps, blocks)):
        plane = CORES * ring(y, step) + (1 - core if flip else core)
        new_jump[at] = block[...]
        new_updated[at] = part[plane] + intensity[0] * block[...]
        for k, (new, out) in enumerate(((new_jump, jump), (new_updated, updated))):
            copy = pltpu.make_async_copy(new.at[at], out.at[plane], done.at[at, k])
            copy.start()
            copies.append(copy)
    for copy in copies:
        copy.wait()


def finish_part(steps, place, intensity, blocks, part, results):
    planes, rows, cols = part.shape
    count = len(steps)
    anywhere = pl.BlockSpec(memory_space=pl.ANY)
    scratch = pltpu.VMEM((count, rows, cols), jnp.float32)
    return pl.pallas_call(
        lambda *refs: finish_kernel(steps, *refs),
        out_shape=[f32(*part.shape)] * 2,
        in_specs=[SMEM, SMEM] + [VMEM] * (count + 1) + [anywhere] * len(results),
        out_specs=[anywhere] * 2, scratch_shapes=[scratch, scratch, pltpu.SemaphoreType.DMA((count, 2))],
        input_output_aliases={count + 3: 0, count + 4: 1} if results else {},
        compiler_params=params(8), name="finish",
    )(place, intensity, *blocks, part, *results)


def neighbours(low_side, high_side, axis):
    count = lax.axis_size(axis)
    forward = [(i, i + 1) for i in range(count - 1)]
    backward = [(i + 1, i) for i in range(count - 1)]
    return lax.ppermute(high_side, axis, forward), lax.ppermute(low_side, axis, backward)


def send(block, move):
    route = []
    for i in range(RING * RING * CORES):
        x, y, core = move(i // (RING * CORES), i // CORES % RING, i % CORES)
        if 0 <= x < RING:
            route.append((i, (x * RING + y % RING) * CORES + core))
    return lax.ppermute(block, "gx", route)


def to_ring(block, step, flip=False):
    return send(block, lambda x, y, core: (x, y + step, 1 - core if flip else core))


def to_other_core(block):
    return send(block, lambda x, y, core: (x, y, 1 - core))


def across_chips(line):
    ends = lax.axis_size("gx") - 1
    route = [(i, i + 1 if i % CORES else i - 1) for i in range(1, ends)]
    return lax.ppermute(line, "gx", route)


def to_group(block, k):
    return send(block, lambda x, y, core: (x + 1 if (y - k) % RING >= RING // 2 else x - 1, y, core))


def after(x, *others):
    return lax.optimization_barrier((x, *others))[0]


def shards(value, kernel_rows, kernel_cols, intensity, diffusion, drift, cross):
    planes, rows, cols = value.shape
    me = lax.axis_index("gx")
    chip = lax.div(me, CORES)
    place = jnp.stack([lax.div(chip, RING), lax.rem(chip, RING), lax.rem(me, CORES)])

    other = to_other_core(value)
    value, high_side, low_side = load_part(place, value)

    s1, s3 = pieces_part((1, 3), place, value, other)
    p0, s2 = pieces_part((0, 2), after(place, s1), value, other)
    p1, p3, x0 = to_ring(s1, 1), to_ring(s3, 3), to_group(p0, 0)
    low, high = neighbours(after(low_side, p0), after(high_side, p0), "gy")
    within, col_hi, col_lo, _ = within_part(value, after(kernel_cols[None], s2))
    taps = taps_part(after(kernel_rows[None], within))
    p2 = to_ring(after(s2, p1, p3, taps[2]), 2)
    x1, x3 = to_group(p1, 1), to_group(p3, 3)
    outer, inner = lines_part(after(place, p1), value, low, high)
    edge, beside = across_chips(outer), to_other_core(inner)
    near = near_part(after(place, outer, x0), p0, p1, p3, taps)
    x2 = to_group(after(p2, near), 2)
    b2, o2 = opposite_part(place, near, p2, x0, x1, x3, taps)
    d2, o2 = to_ring(b2, -2), to_ring(o2, -2, True)
    b0, o0, b1, o1, b3, o3 = others_part(place, near, p2, x0, x1, x2, x3, taps)
    d1, d3 = to_ring(b1, -1), to_ring(b3, -3)
    o1, o3 = to_ring(o1, -1, True), to_ring(o3, -3, True)
    o0 = to_other_core(o0)
    jump_cols, part = local_part(
        place, after(intensity, b0), diffusion, drift, cross, value, low, high, beside, edge, within, (col_hi, col_lo)
    )
    results = finish_part(((0, 0), (0, 1), (2, 0), (2, 1)), place, intensity, (b0, o0, d2, o2), part, ())
    results = finish_part(((1, 0), (3, 0)), place, intensity, (d1, d3), part, results)
    updated, jump_rows = finish_part(((1, 1), (3, 1)), place, intensity, (o1, o3), part, results)
    return updated, jump_rows, jump_cols


def solution(mesh):
    return jax.shard_map(
        shards,
        mesh=mesh,
        in_specs=(P(None, "gx", "gy"), P(), P(), P(), P(), P(), P()),
        out_specs=(P(None, "gx", "gy"), P(None, "gx", "gy"), P(None, "gx", "gy")),
        check_vma=False,
    )
```
